768 devices in a mesh: grp: 8 (over y), peer: 96 (over z, x, core).
Axes of the slice: x: 4, y: 8, z: 12, core: 2. Of those that a mesh axis runs over, the one named last changes fastest.
Arguments:
- state: float32 [393216, 288], P(('grp', 'peer')), may hold values from -6 to 6
- cost: int32 [393216], P(('grp', 'peer')), may hold values from 0 to 48, as said below
- links: int32 [768, 64], P(('grp', 'peer')), may hold values from 0 to 63, each once within a row
- dyn_weight: bfloat16 [288, 288], replicated, may hold values from -0.375 to 0.375
- rad_weight: bfloat16 [288, 288], replicated, may hold values from -0.375 to 0.375
- cloud_weight: bfloat16 [288, 288], replicated, may hold values from -0.375 to 0.375
Outputs:
- state_next: float32 [393216, 288], P(('grp', 'peer'))
The draws below stay inside these ranges and needn't reach their ends.
Inputs may be any that keep to these rules, and one draw needn't show every extreme that they name: A column is cloudy where its cost is above 0. A block of 512 consecutive columns holds at most 192 cloudy columns; every aligned group of 96 such blocks holds exactly 4608 cloudy columns, and one block of each group exactly 192. `links`: each row is a permutation of 0 to 63.
All inputs are finite; a program needn't handle non-finite values.
Results may differ from the reference program's by a relative error of at most 0.0039.
Values may be sent and summed in bfloat16 or wider, within the bound.
A program may use at most 32 MiB of HBM per device.

```python
import jax
import jax.numpy as jnp
from jax import lax

LEV = 48
COLS = 512
SPAN = 48
EDGE = 64
MICRO = 24
SUBSTEPS = 3
FL = 288
NCOL = 393216
CLOUDY_ALL = 36864
N_GRP = 8
N_PEER = 96


def draw_cost(key, part):
    key = jax.random.fold_in(key, 7)
    key_order, key_share, key_pick, key_depth = jax.random.split(key, 4)
    block_count = NCOL // COLS
    group_count = block_count // N_PEER
    quarters = N_PEER // 4
    share = jax.random.randint(key_share, (group_count, quarters), 0, SPAN + 1)
    share = share.at[:, 0].set(SPAN)
    heavy = SPAN + 3 * share
    light = SPAN - share
    counts = jnp.concatenate([heavy[:, :, None], jnp.broadcast_to(light[:, :, None], (group_count, quarters, 3))], axis=2)
    counts = counts.reshape(group_count, N_PEER)
    shuffle = jax.vmap(lambda one: jax.random.permutation(one, N_PEER))(jax.random.split(key_pick, group_count))
    counts = jnp.take_along_axis(counts, shuffle, axis=1).reshape(block_count)
    ranking = jax.vmap(lambda one: jax.random.permutation(one, COLS))(jax.random.split(key_order, block_count))
    cloud_depth = jax.random.randint(key_depth, (block_count, COLS), 1, LEV + 1)
    cloud_depth = jnp.where(ranking == 0, LEV, cloud_depth)
    result = jnp.where(ranking < counts[:, None], cloud_depth, 0)
    return result.reshape(NCOL).astype(jnp.int32)


def shard_levels(own_key, dims, cuts, smallest, high):
    loudness = 1.0
    for axis_at, parts in cuts:
        steps = jax.random.uniform(jax.random.fold_in(jax.random.fold_in(own_key, 6), axis_at), (parts,), jnp.float32, smallest / len(cuts), high / len(cuts))
        loudness = loudness * jnp.repeat(jnp.exp(steps), dims[axis_at] // parts).reshape((-1,) + (1,) * (len(dims) - 1 - axis_at))
    return loudness


def gaussian(rng, extent, scale, limit, cuts=(), kind=jnp.bfloat16):
    factor_of = shard_levels(rng, extent, cuts, -0.22, 0.18) if cuts else 1.0
    array = jax.random.normal(rng, extent, jnp.float32) * scale * factor_of
    return jnp.minimum(jnp.maximum(array, -limit), limit).astype(kind)


def setup_inputs(seed: int = 0) -> dict:
    splits = jax.random.split(jax.random.key(seed), 7)
    state = gaussian(splits[0], (NCOL, FL), 1.0, 6.0, ((0, 768),), jnp.float32)
    cost = draw_cost(jax.random.fold_in(splits[6], 71), 0)
    links = jax.vmap(lambda own: jax.random.permutation(own, EDGE))(jax.random.split(splits[2], (N_GRP * N_PEER))).reshape((N_GRP * N_PEER, EDGE)).astype(jnp.int32)
    dyn_weight = gaussian(splits[3], (FL, FL), FL ** -0.5, 0.375)
    rad_weight = gaussian(splits[4], (FL, FL), FL ** -0.5, 0.375)
    cloud_weight = gaussian(splits[5], (FL, FL), FL ** -0.5, 0.375)
    return {"state": state, "cost": cost, "links": links, "dyn_weight": dyn_weight, "rad_weight": rad_weight, "cloud_weight": cloud_weight}


def cloud_physics(rows_in, cloud_depth, cloud_weight):
    level_index = jnp.arange(FL, dtype=jnp.int32) % LEV
    level_mask = (level_index[None, :] >= (LEV - cloud_depth)[:, None]).astype(jnp.float32)
    initial = rows_in.astype(jnp.float32)

    def micro_turn(count, iterate):
        forcing = jnp.tanh(jnp.dot(iterate.astype(jnp.bfloat16), cloud_weight, preferred_element_type=jnp.float32))
        return iterate + 0.1 * level_mask * forcing

    finished = lax.fori_loop(0, MICRO, micro_turn, initial)
    return (finished - initial).astype(jnp.bfloat16)


def edge_average(column_state, links):
    block_count = column_state.shape[0]
    left_rim = column_state[:, :EDGE]
    right_rim = column_state[:, COLS - EDGE:]
    prev_right = jnp.roll(right_rim, 1, axis=0)
    matched = jnp.take_along_axis(prev_right, links[:, :, None], axis=1)
    new_left = 0.5 * (left_rim + matched)
    next_links = jnp.roll(links, -1, axis=0)
    block_index = jnp.arange(block_count, dtype=jnp.int32)[:, None]
    new_right = jnp.zeros_like(right_rim).at[block_index, next_links].set(jnp.roll(new_left, -1, axis=0))
    return column_state.at[:, :EDGE].set(new_left).at[:, COLS - EDGE:].set(new_right)


def reference(state, cost, links, dyn_weight, rad_weight, cloud_weight):
    initial = state.astype(jnp.bfloat16)
    heating = jnp.dot(initial, rad_weight, preferred_element_type=jnp.float32)
    cloudy = jnp.nonzero(cost > 0, size=CLOUDY_ALL, fill_value=0)[0].astype(jnp.int32)
    change = cloud_physics(initial[cloudy], cost[cloudy], cloud_weight)
    cloud_change = jnp.zeros((NCOL, FL), jnp.float32).at[cloudy].set(change.astype(jnp.float32))
    block_count = NCOL // COLS
    column_state = state
    for substep in range(SUBSTEPS):
        column_state = column_state + 0.2 * jnp.dot(column_state.astype(jnp.bfloat16), dyn_weight, preferred_element_type=jnp.float32)
        column_state = edge_average(column_state.reshape(block_count, COLS, FL), links).reshape(NCOL, FL)
    return column_state + 0.25 * heating + cloud_change
```

```python
import functools

import jax
import jax.numpy as jnp
from jax import lax
from jax.experimental import pallas as pl
from jax.experimental.pallas import tpu as pltpu
from jax.sharding import PartitionSpec as P

LEV = 48
SLOTS = 256
EDGE = 64
MICRO = 24
LANES = 128
MESH = pl.DeviceIdType.MESH
F32 = jnp.float32
BF16 = jnp.bfloat16


def mm(a, b):
    return lax.dot_general(a, b, (((1,), (0,)), ((), ())), preferred_element_type=F32)


def mm_nt(a, b):
    return lax.dot_general(a, b, (((1,), (1,)), ((), ())), preferred_element_type=F32)


def one_hot(condition):
    return jnp.where(condition, 1.0, 0.0).astype(BF16)


def iota(shape, dim):
    return lax.broadcasted_iota(jnp.int32, shape, dim)


def kernel(
    n_grp, n_peer,
    x_hbm, cost_hbm, links_hbm, wd_hbm, wr_hbm, wc_hbm,
    out,
    x, cost, links, wd, wr, wc,
    xb, wct, wdr, dt, pt, first, now, mask, rim_out, rim_in, edge_out, edge_in,
    load_sem, send_sem, recv_sem,
):
    width, cols = x.shape
    tiles = cols // LANES
    half = width // 2
    flat = lax.axis_index("grp") * n_peer + lax.axis_index("peer")
    count = n_grp * n_peer
    right = lax.rem(flat + 1, count)
    left = lax.rem(flat + count - 1, count)
    right_id = (lax.div(right, n_peer), lax.rem(right, n_peer))
    left_id = (lax.div(left, n_peer), lax.rem(left, n_peer))

    def lane_tile(t):
        return pl.ds(t * LANES, LANES)

    loads = {}
    order = [tiles - 1, 0] + list(range(1, tiles - 1))
    for t in order[:1]:
        loads[t] = pltpu.make_async_copy(x_hbm.at[:, lane_tile(t)], x.at[:, lane_tile(t)], load_sem.at[t])
        loads[t].start()

    barrier = pltpu.get_barrier_semaphore()
    pl.semaphore_signal(barrier, inc=1, device_id=left_id, device_id_type=MESH)

    for k, (src, dst) in enumerate(((links_hbm, links), (cost_hbm, cost))):
        loads["links" if k == 0 else "cost"] = pltpu.make_async_copy(src, dst, load_sem.at[tiles + k])
        loads["links" if k == 0 else "cost"].start()
    for t in order[1:]:
        loads[t] = pltpu.make_async_copy(x_hbm.at[:, lane_tile(t)], x.at[:, lane_tile(t)], load_sem.at[t])
        loads[t].start()
    for k, (name, src, dst) in enumerate((("wc", wc_hbm, wc), ("wd", wd_hbm, wd), ("wr", wr_hbm, wr))):
        loads[name] = pltpu.make_async_copy(src, dst, load_sem.at[tiles + 2 + k])
        loads[name].start()

    last = lane_tile(tiles - 1)
    loads[tiles - 1].wait()
    upper = pltpu.roll(x[:half, last], EDGE, 1)
    lower = x[half:, last]
    rim_out[...] = jnp.where(iota((half, LANES), 1) < EDGE, upper, lower).astype(BF16)
    pl.semaphore_wait(barrier, 1)
    forward = pltpu.make_async_remote_copy(
        src_ref=rim_out, dst_ref=rim_in, send_sem=send_sem.at[0], recv_sem=recv_sem.at[0],
        device_id=right_id, device_id_type=MESH,
    )
    forward.start()

    loads["links"].wait()
    link_row = jnp.concatenate([links[...], jnp.full((1, LANES - EDGE), -LANES, jnp.int32)], axis=1)
    rows_at = iota((LANES, LANES), 0)
    match_top = one_hot(rows_at == link_row)
    match_bottom = one_hot(rows_at - EDGE == link_row)

    for t in range(tiles):
        if t < tiles - 1:
            loads[t].wait()
        xb[:width, lane_tile(t)] = x[:, lane_tile(t)].astype(BF16)
    edge_out[...] = (
        mm_nt(xb[:half, :LANES], match_top) + mm_nt(xb[half:width, :LANES], match_bottom)
    ).astype(BF16)

    loads["cost"].wait()
    depth_row = cost[...]
    xb[width:, :] = jnp.broadcast_to(depth_row.astype(F32), (xb.shape[0] - width, cols)).astype(BF16)
    cloudy = jnp.where(depth_row > 0, 1.0, 0.0)
    cloudy_rows = jnp.broadcast_to(cloudy, (16, cols)).astype(BF16)
    ahead = one_hot(iota((LANES, LANES), 0) < iota((LANES, LANES), 1))
    before = jnp.zeros((1, 1), F32)
    for t in range(tiles):
        here = cloudy[:, t * LANES:(t + 1) * LANES]
        rank = mm(cloudy_rows[:, t * LANES:(t + 1) * LANES], ahead)[:1] + before
        before = before + jnp.sum(here, axis=1, keepdims=True)
        place = jnp.where(here > 0, rank.astype(jnp.int32), -1)
        pt[:, lane_tile(t)] = one_hot(iota((SLOTS, LANES), 0) == place)

    eye = one_hot(iota((width, width), 0) == iota((width, width), 1))
    loads["wc"].wait()
    wct[...] = mm_nt(eye, wc[...]).astype(BF16)

    gathered = mm_nt(xb[...], pt[...])
    first[...] = gathered[:width]
    now[...] = gathered[:width]
    slot_depth = gathered[width:width + 1].astype(jnp.int32)
    level = lax.rem(iota((width, SLOTS), 0), LEV)
    mask[...] = jnp.where(level >= LEV - slot_depth, 0.1, 0.0)

    def micro_turn(i, carry):
        forcing = mm(wct[...], now[...].astype(BF16))
        now[...] = now[...] + mask[...] * jnp.tanh(forcing)
        return carry

    lax.fori_loop(0, MICRO, micro_turn, 0)
    change = (now[...] - first[...]).astype(BF16)

    loads["wd"].wait()
    loads["wr"].wait()
    wdr[:width] = mm_nt(eye, wd[...]).astype(BF16)
    wdr[width:] = mm_nt(eye, wr[...]).astype(BF16)
    wdt = wdr[:width]
    two = mm(wdt, wdt)
    three = mm(wdt, two.astype(BF16))
    dt[...] = (0.6 * wdt.astype(F32) + 0.12 * two + 0.008 * three).astype(BF16)

    for t in range(tiles):
        at = lane_tile(t)
        both = mm(wdr[...], xb[:width, at])
        turned = x[:, at] + 0.2 * both[:width]
        rest = 0.25 * both[width:] + mm(change, pt[:, at])
        for _ in range(2):
            turned = turned + 0.2 * mm(wdr[:width], turned.astype(BF16))
        lane = iota((width, LANES), 1)
        if t == 0:
            turned = jnp.where(lane < EDGE, 0.5 * turned, turned)
        if t == tiles - 1:
            turned = jnp.where(lane >= EDGE, 0.5 * turned, turned)
        out[:, at] = turned + rest

    forward.wait_recv()
    backward = pltpu.make_async_remote_copy(
        src_ref=edge_out, dst_ref=edge_in, send_sem=send_sem.at[1], recv_sem=recv_sem.at[1],
        device_id=left_id, device_id_type=MESH,
    )
    backward.start()
    matched = jnp.concatenate([mm(rim_in[...], match_top), mm(rim_in[...], match_bottom)], axis=0)
    out[:, :LANES] = out[:, :LANES] + 0.5 * (matched + mm(dt[...], matched.astype(BF16)))

    backward.wait_recv()
    into_top = one_hot((iota((LANES, LANES), 0) + EDGE == iota((LANES, LANES), 1)))
    into_bottom = one_hot((iota((LANES, LANES), 0) == iota((LANES, LANES), 1)) & (iota((LANES, LANES), 0) >= EDGE))
    matched = jnp.concatenate([mm(edge_in[...], into_top), mm(edge_in[...], into_bottom)], axis=0)
    out[:, last] = out[:, last] + 0.5 * (matched + mm(dt[...], matched.astype(BF16)))
    forward.wait_send()
    backward.wait_send()


def solution(mesh):
    n_grp, n_peer = mesh.shape["grp"], mesh.shape["peer"]

    def per_device(state, cost, links, dyn_weight, rad_weight, cloud_weight):
        cols, width = state.shape
        half = width // 2
        tiles = cols // LANES
        flipped = pl.pallas_call(
            functools.partial(kernel, n_grp, n_peer),
            out_shape=jax.ShapeDtypeStruct((width, cols), F32),
            in_specs=[pl.BlockSpec(memory_space=pltpu.HBM)] * 6,
            out_specs=pl.BlockSpec(memory_space=pltpu.VMEM),
            scratch_shapes=[
                pltpu.VMEM((width, cols), F32),
                pltpu.VMEM((1, cols), jnp.int32),
                pltpu.VMEM((1, EDGE), jnp.int32),
                pltpu.VMEM((width, width), BF16),
                pltpu.VMEM((width, width), BF16),
                pltpu.VMEM((width, width), BF16),
                pltpu.VMEM((width + 16, cols), BF16),
                pltpu.VMEM((width, width), BF16),
                pltpu.VMEM((2 * width, width), BF16),
                pltpu.VMEM((width, width), BF16),
                pltpu.VMEM((SLOTS, cols), BF16),
                pltpu.VMEM((width, SLOTS), F32),
                pltpu.VMEM((width, SLOTS), F32),
                pltpu.VMEM((width, SLOTS), F32),
                pltpu.VMEM((half, LANES), BF16),
                pltpu.VMEM((half, LANES), BF16),
                pltpu.VMEM((half, LANES), BF16),
                pltpu.VMEM((half, LANES), BF16),
                pltpu.SemaphoreType.DMA((tiles + 5,)),
                pltpu.SemaphoreType.DMA((2,)),
                pltpu.SemaphoreType.DMA((2,)),
            ],
            compiler_params=pltpu.CompilerParams(
                collective_id=0, has_side_effects=True, vmem_limit_bytes=32 * 2**20
            ),
        )(state.T, cost.reshape(1, cols), links, dyn_weight, rad_weight, cloud_weight)
        return flipped.T

    return jax.shard_map(
        per_device,
        mesh=mesh,
        in_specs=(
            P(("grp", "peer"), None),
            P(("grp", "peer")),
            P(("grp", "peer"), None),
            P(),
            P(),
            P(),
        ),
        out_specs=P(("grp", "peer"), None),
        check_vma=False,
    )
```

```python
import functools

import jax
import jax.numpy as jnp
from jax import lax
from jax.experimental import pallas as pl
from jax.experimental.pallas import tpu as pltpu
from jax.sharding import PartitionSpec as P

LEV = 48
SLOTS = 256
EDGE = 64
MICRO = 24
LANES = 128
WIDE = 256
PIECES = 3
MESH = pl.DeviceIdType.MESH
F32 = jnp.float32
BF16 = jnp.bfloat16


def mm(a, b):
    return lax.dot_general(a, b, (((1,), (0,)), ((), ())), preferred_element_type=F32)


def mm_nt(a, b):
    return lax.dot_general(a, b, (((1,), (1,)), ((), ())), preferred_element_type=F32)


def one_hot(condition):
    return jnp.where(condition, 1.0, 0.0).astype(BF16)


def iota(shape, dim):
    return lax.broadcasted_iota(jnp.int32, shape, dim)


def kernel(
    n_grp, n_peer,
    x_hbm, cost_hbm, links_hbm, wd_hbm, wr_hbm, wc_hbm,
    out,
    x, cost, links, wd, wr, wc,
    xb, wct, wdr, dt, pt, match, first, now, mask, rim_out, rim_in, edge_out, edge_in,
    rim_sem, load_sem, send_sem, recv_sem, ready_sem,
):
    width, cols = x.shape
    first_peer = lax.axis_index("peer") == 0
    tiles = cols // LANES
    half = width // 2
    flat = lax.axis_index("grp") * n_peer + lax.axis_index("peer")
    count = n_grp * n_peer
    right = lax.rem(flat + 1, count)
    left = lax.rem(flat + count - 1, count)
    right_id = (lax.div(right, n_peer), lax.rem(right, n_peer))
    left_id = (lax.div(left, n_peer), lax.rem(left, n_peer))

    def lane_tile(t):
        return pl.ds(t * LANES, LANES)

    last = lane_tile(tiles - 1)
    piece = half // PIECES
    pieces = [pl.ds(k * piece, piece) for k in range(PIECES)]
    rim_loads = []
    for k in range(PIECES):
        for side in range(2):
            rows = pl.ds(side * half + k * piece, piece)
            rim_loads.append(pltpu.make_async_copy(x_hbm.at[rows, last], x.at[rows, last], rim_sem.at[2 * k + side]))
            rim_loads[-1].start()

    barrier = pltpu.get_barrier_semaphore()
    pl.semaphore_signal(barrier, inc=1, device_id=left_id, device_id_type=MESH)

    loads = {}
    for k, (name, src, dst) in enumerate((
        ("links", links_hbm, links),
        (0, x_hbm.at[:, lane_tile(0)], x.at[:, lane_tile(0)]),
        ("cost", cost_hbm, cost),
        (1, x_hbm.at[:, pl.ds(LANES, cols - 2 * LANES)], x.at[:, pl.ds(LANES, cols - 2 * LANES)]),
        ("wc", wc_hbm, wc),
        ("wd", wd_hbm, wd),
        ("wr", wr_hbm, wr),
    )):
        loads[name] = pltpu.make_async_copy(src, dst, load_sem.at[k])
        loads[name].start()

    pl.semaphore_wait(barrier, 1)
    pl.semaphore_signal(ready_sem, inc=1, device_id=right_id, device_id_type=MESH)

    forward = []
    for k in range(PIECES):
        rim_loads[2 * k].wait()
        rim_loads[2 * k + 1].wait()
        upper = pltpu.roll(x[pieces[k], last], EDGE, 1)
        lower = x[pl.ds(half + k * piece, piece), last]
        rim_out[pieces[k]] = jnp.where(iota((piece, LANES), 1) < EDGE, upper, lower).astype(BF16)
        forward.append(pltpu.make_async_remote_copy(
            src_ref=rim_out.at[pieces[k]], dst_ref=rim_in.at[pieces[k]],
            send_sem=send_sem.at[k], recv_sem=recv_sem.at[k],
            device_id=right_id, device_id_type=MESH,
        ))
        forward[k].start()
    backward = pltpu.make_async_remote_copy(
        src_ref=edge_out, dst_ref=edge_in, send_sem=send_sem.at[PIECES], recv_sem=recv_sem.at[PIECES],
        device_id=left_id, device_id_type=MESH,
    )

    loads["links"].wait()
    link_row = jnp.concatenate([links[...], jnp.full((1, LANES - EDGE), -LANES, jnp.int32)], axis=1)
    rows_at = iota((LANES, LANES), 0)
    match[:, :LANES] = one_hot(rows_at == link_row)
    match[:, LANES:] = one_hot(rows_at - EDGE == link_row)

    loads[0].wait()
    xb[:width, :LANES] = x[:, :LANES].astype(BF16)
    edge_out[...] = (
        mm_nt(xb[:half, :LANES], match[:, :LANES]) + mm_nt(xb[half:width, :LANES], match[:, LANES:])
    ).astype(BF16)
    loads[1].wait()
    for t in range(1, tiles):
        xb[:width, lane_tile(t)] = x[:, lane_tile(t)].astype(BF16)

    loads["cost"].wait()
    depth_row = cost[...]
    xb[width:, :] = jnp.broadcast_to(depth_row.astype(F32), (xb.shape[0] - width, cols)).astype(BF16)
    cloudy = jnp.where(depth_row > 0, 1.0, 0.0)
    cloudy_rows = jnp.broadcast_to(cloudy, (16, cols)).astype(BF16)
    ahead = one_hot(iota((LANES, LANES), 0) < iota((LANES, LANES), 1))
    before = jnp.zeros((1, 1), F32)
    for t in range(tiles):
        here = cloudy[:, t * LANES:(t + 1) * LANES]
        rank = mm(cloudy_rows[:, t * LANES:(t + 1) * LANES], ahead)[:1] + before
        before = before + jnp.sum(here, axis=1, keepdims=True)
        place = jnp.where(here > 0, rank.astype(jnp.int32), -1)
        pt[:, lane_tile(t)] = one_hot(iota((SLOTS, LANES), 0) == place)

    eye = one_hot(iota((width, width), 0) == iota((width, width), 1))
    loads["wc"].wait()
    wct[...] = mm_nt(eye, wc[...]).astype(BF16)

    gathered = mm_nt(xb[...], pt[...])
    first[...] = gathered[:width]
    now[...] = gathered[:width]
    slot_depth = gathered[width:width + 1].astype(jnp.int32)
    level = lax.rem(iota((width, SLOTS), 0), LEV)
    mask[...] = jnp.where(level >= LEV - slot_depth, 0.1, 0.0)

    def micro_turn(i, carry):
        forcing = mm(wct[...], now[...].astype(BF16))
        now[...] = now[...] + mask[...] * jnp.tanh(forcing)
        return carry

    lax.fori_loop(0, MICRO, micro_turn, 0)
    change = (now[...] - first[...]).astype(BF16)

    @pl.when(jnp.logical_not(first_peer))
    def _():
        pl.semaphore_wait(ready_sem, 1)
        backward.start()

    loads["wd"].wait()
    loads["wr"].wait()
    wdr[:width] = mm_nt(eye, wd[...]).astype(BF16)
    wdr[width:] = mm_nt(eye, wr[...]).astype(BF16)
    wdt = wdr[:width]
    two = mm(wdt, wdt)
    three = mm(wdt, two.astype(BF16))
    dt[...] = (0.6 * wdt.astype(F32) + 0.12 * two + 0.008 * three).astype(BF16)

    for t in range(cols // WIDE):
        at = pl.ds(t * WIDE, WIDE)
        both = mm(wdr[...], xb[:width, at])
        turned = x[:, at] + 0.2 * both[:width]
        rest = 0.25 * both[width:] + mm(change, pt[:, at])
        for _ in range(2):
            turned = turned + 0.2 * mm(wdr[:width], turned.astype(BF16))
        column = iota((width, WIDE), 1) + t * WIDE
        turned = jnp.where((column < EDGE) | (column >= cols - EDGE), 0.5 * turned, turned)
        out[:, at] = turned + rest

    backward.wait_recv()
    above, across = iota((LANES, LANES), 0), iota((LANES, LANES), 1)
    into_top = one_hot(above + EDGE == across)
    into_bottom = one_hot((above == across) & (above >= EDGE))
    matched = jnp.concatenate([mm(edge_in[...], into_top), mm(edge_in[...], into_bottom)], axis=0)
    out[:, last] = out[:, last] + 0.5 * (matched + mm(dt[...], matched.astype(BF16)))

    @pl.when(first_peer)
    def _():
        pl.semaphore_wait(ready_sem, 1)
        backward.start()

    for copy in forward:
        copy.wait_recv()
    halves = mm(rim_in[...], match[...])
    matched = jnp.concatenate([halves[:, :LANES], halves[:, LANES:]], axis=0)
    out[:, :LANES] = out[:, :LANES] + 0.5 * (matched + mm(dt[...], matched.astype(BF16)))
    for copy in forward:
        copy.wait_send()
    backward.wait_send()


def solution(mesh):
    n_grp, n_peer = mesh.shape["grp"], mesh.shape["peer"]

    def per_device(state, cost, links, dyn_weight, rad_weight, cloud_weight):
        cols, width = state.shape
        half = width // 2
        held = [state.T, cost.reshape(1, cols), links, dyn_weight, rad_weight, cloud_weight]
        held = [pltpu.with_memory_space_constraint(one, pltpu.HBM) for one in held]
        flipped = pl.pallas_call(
            functools.partial(kernel, n_grp, n_peer),
            out_shape=jax.ShapeDtypeStruct((width, cols), F32),
            in_specs=[pl.BlockSpec(memory_space=pltpu.HBM)] * 6,
            out_specs=pl.BlockSpec(memory_space=pltpu.VMEM),
            scratch_shapes=[
                pltpu.VMEM((width, cols), F32),
                pltpu.VMEM((1, cols), jnp.int32),
                pltpu.VMEM((1, EDGE), jnp.int32),
                pltpu.VMEM((width, width), BF16),
                pltpu.VMEM((width, width), BF16),
                pltpu.VMEM((width, width), BF16),
                pltpu.VMEM((width + 16, cols), BF16),
                pltpu.VMEM((width, width), BF16),
                pltpu.VMEM((2 * width, width), BF16),
                pltpu.VMEM((width, width), BF16),
                pltpu.VMEM((SLOTS, cols), BF16),
                pltpu.VMEM((LANES, 2 * LANES), BF16),
                pltpu.VMEM((width, SLOTS), F32),
                pltpu.VMEM((width, SLOTS), F32),
                pltpu.VMEM((width, SLOTS), F32),
                pltpu.VMEM((half, LANES), BF16),
                pltpu.VMEM((half, LANES), BF16),
                pltpu.VMEM((half, LANES), BF16),
                pltpu.VMEM((half, LANES), BF16),
                pltpu.SemaphoreType.DMA((2 * PIECES,)),
                pltpu.SemaphoreType.DMA((7,)),
                pltpu.SemaphoreType.DMA((PIECES + 1,)),
                pltpu.SemaphoreType.DMA((PIECES + 1,)),
                pltpu.SemaphoreType.REGULAR,
            ],
            compiler_params=pltpu.CompilerParams(
                collective_id=0, has_side_effects=True, vmem_limit_bytes=32 * 2**20
            ),
        )(*held)
        return flipped.T

    return jax.shard_map(
        per_device,
        mesh=mesh,
        in_specs=(
            P(("grp", "peer"), None),
            P(("grp", "peer")),
            P(("grp", "peer"), None),
            P(),
            P(),
            P(),
        ),
        out_specs=P(("grp", "peer"), None),
        check_vma=False,
    )
```

```python
import functools

import jax
import jax.numpy as jnp
from jax import lax
from jax.experimental import pallas as pl
from jax.experimental.pallas import tpu as pltpu
from jax.sharding import PartitionSpec as P

LEV = 48
SLOTS = 256
EDGE = 64
MICRO = 24
LANES = 128
WIDE = 256
PIECES = 3
MESH = pl.DeviceIdType.MESH
F32 = jnp.float32
BF16 = jnp.bfloat16


def mm(a, b):
    return lax.dot_general(a, b, (((1,), (0,)), ((), ())), preferred_element_type=F32)


def mm_nt(a, b):
    return lax.dot_general(a, b, (((1,), (1,)), ((), ())), preferred_element_type=F32)


def one_hot(condition):
    return jnp.where(condition, 1.0, 0.0).astype(BF16)


def iota(shape, dim):
    return lax.broadcasted_iota(jnp.int32, shape, dim)


def kernel(
    n_grp, n_peer,
    x_hbm, cost_hbm, links_hbm, wd_hbm, wr_hbm, wc_hbm,
    out, came, spot, dt,
    x, cost, links, wd, wr, wc,
    xb, wct, wdr, pt, first, now, mask, rim_out, rim_in, edge_out, edge_in,
    rim_sem, load_sem, send_sem, recv_sem, ready_sem,
):
    width, cols = x.shape
    first_peer = lax.axis_index("peer") == 0
    tiles = cols // LANES
    half = width // 2
    flat = lax.axis_index("grp") * n_peer + lax.axis_index("peer")
    count = n_grp * n_peer
    right = lax.rem(flat + 1, count)
    left = lax.rem(flat + count - 1, count)
    right_id = (lax.div(right, n_peer), lax.rem(right, n_peer))
    left_id = (lax.div(left, n_peer), lax.rem(left, n_peer))

    def lane_tile(t):
        return pl.ds(t * LANES, LANES)

    last = lane_tile(tiles - 1)
    piece = half // PIECES
    pieces = [pl.ds(k * piece, piece) for k in range(PIECES)]
    rim_loads = []
    for k in range(PIECES):
        for side in range(2):
            rows = pl.ds(side * half + k * piece, piece)
            rim_loads.append(pltpu.make_async_copy(x_hbm.at[rows, last], x.at[rows, last], rim_sem.at[2 * k + side]))
            rim_loads[-1].start()

    barrier = pltpu.get_barrier_semaphore()
    pl.semaphore_signal(barrier, inc=1, device_id=left_id, device_id_type=MESH)

    loads = {}
    for k, (name, src, dst) in enumerate((
        ("links", links_hbm, links),
        (0, x_hbm.at[:, lane_tile(0)], x.at[:, lane_tile(0)]),
        ("cost", cost_hbm, cost),
        (1, x_hbm.at[:, pl.ds(LANES, cols - 2 * LANES)], x.at[:, pl.ds(LANES, cols - 2 * LANES)]),
        ("wc", wc_hbm, wc),
        ("wd", wd_hbm, wd),
        ("wr", wr_hbm, wr),
    )):
        loads[name] = pltpu.make_async_copy(src, dst, load_sem.at[k])
        loads[name].start()

    pl.semaphore_wait(barrier, 1)
    pl.semaphore_signal(ready_sem, inc=1, device_id=right_id, device_id_type=MESH)

    forward = []
    for k in range(PIECES):
        rim_loads[2 * k].wait()
        rim_loads[2 * k + 1].wait()
        upper = pltpu.roll(x[pieces[k], last], EDGE, 1)
        lower = x[pl.ds(half + k * piece, piece), last]
        rim_out[pieces[k]] = jnp.where(iota((piece, LANES), 1) < EDGE, upper, lower).astype(BF16)
        forward.append(pltpu.make_async_remote_copy(
            src_ref=rim_out.at[pieces[k]], dst_ref=rim_in.at[pieces[k]],
            send_sem=send_sem.at[k], recv_sem=recv_sem.at[k],
            device_id=right_id, device_id_type=MESH,
        ))
        forward[k].start()
    backward = pltpu.make_async_remote_copy(
        src_ref=edge_out, dst_ref=edge_in, send_sem=send_sem.at[PIECES], recv_sem=recv_sem.at[PIECES],
        device_id=left_id, device_id_type=MESH,
    )

    loads["links"].wait()
    link_row = jnp.concatenate([links[...], jnp.full((1, LANES - EDGE), -LANES, jnp.int32)], axis=1)
    rows_at = iota((LANES, LANES), 0)
    match_top = one_hot(rows_at == link_row)
    match_bottom = one_hot(rows_at - EDGE == link_row)
    spot[...] = jnp.concatenate([links[...], links[...] + EDGE], axis=1)

    loads[0].wait()
    xb[:width, :LANES] = x[:, :LANES].astype(BF16)
    edge_out[...] = (
        mm_nt(xb[:half, :LANES], match_top) + mm_nt(xb[half:width, :LANES], match_bottom)
    ).astype(BF16)
    loads[1].wait()
    for t in range(1, tiles):
        xb[:width, lane_tile(t)] = x[:, lane_tile(t)].astype(BF16)

    loads["cost"].wait()
    depth_row = cost[...]
    xb[width:, :] = jnp.broadcast_to(depth_row.astype(F32), (xb.shape[0] - width, cols)).astype(BF16)
    cloudy = jnp.where(depth_row > 0, 1.0, 0.0)
    cloudy_rows = jnp.broadcast_to(cloudy, (16, cols)).astype(BF16)
    ahead = one_hot(iota((LANES, LANES), 0) < iota((LANES, LANES), 1))
    before = jnp.zeros((1, 1), F32)
    for t in range(tiles):
        here = cloudy[:, t * LANES:(t + 1) * LANES]
        rank = mm(cloudy_rows[:, t * LANES:(t + 1) * LANES], ahead)[:1] + before
        before = before + jnp.sum(here, axis=1, keepdims=True)
        place = jnp.where(here > 0, rank.astype(jnp.int32), -1)
        pt[:, lane_tile(t)] = one_hot(iota((SLOTS, LANES), 0) == place)

    eye = one_hot(iota((width, width), 0) == iota((width, width), 1))
    loads["wc"].wait()
    wct[...] = mm_nt(eye, wc[...]).astype(BF16)

    gathered = mm_nt(xb[...], pt[...])
    first[...] = gathered[:width]
    now[...] = gathered[:width]
    slot_depth = gathered[width:width + 1].astype(jnp.int32)
    level = lax.rem(iota((width, SLOTS), 0), LEV)
    mask[...] = jnp.where(level >= LEV - slot_depth, 0.1, 0.0)

    def micro_turn(i, carry):
        forcing = mm(wct[...], now[...].astype(BF16))
        now[...] = now[...] + mask[...] * jnp.tanh(forcing)
        return carry

    lax.fori_loop(0, MICRO, micro_turn, 0)
    change = (now[...] - first[...]).astype(BF16)

    @pl.when(jnp.logical_not(first_peer))
    def _():
        pl.semaphore_wait(ready_sem, 1)
        backward.start()

    loads["wd"].wait()
    loads["wr"].wait()
    wdr[:width] = mm_nt(eye, wd[...]).astype(BF16)
    wdr[width:] = mm_nt(eye, wr[...]).astype(BF16)
    wdt = wdr[:width]
    two = mm(wdt, wdt)
    three = mm(wdt, two.astype(BF16))
    dt[...] = (0.6 * wdt.astype(F32) + 0.12 * two + 0.008 * three).astype(BF16)

    for t in range(cols // WIDE):
        at = pl.ds(t * WIDE, WIDE)
        both = mm(wdr[...], xb[:width, at])
        turned = x[:, at] + 0.2 * both[:width]
        rest = 0.25 * both[width:] + mm(change, pt[:, at])
        for _ in range(2):
            turned = turned + 0.2 * mm(wdr[:width], turned.astype(BF16))
        column = iota((width, WIDE), 1) + t * WIDE
        turned = jnp.where((column < EDGE) | (column >= cols - EDGE), 0.5 * turned, turned)
        out[:, at] = turned + rest

    backward.wait_recv()
    above, across = iota((LANES, LANES), 0), iota((LANES, LANES), 1)
    into_top = one_hot(above + EDGE == across)
    into_bottom = one_hot((above == across) & (above >= EDGE))
    matched = jnp.concatenate([mm(edge_in[...], into_top), mm(edge_in[...], into_bottom)], axis=0)
    out[:, last] = out[:, last] + 0.5 * (matched + mm(dt[...], matched.astype(BF16)))

    @pl.when(first_peer)
    def _():
        pl.semaphore_wait(ready_sem, 1)
        backward.start()

    for copy in forward:
        copy.wait_recv()
    came[...] = rim_in[...]
    for copy in forward:
        copy.wait_send()
    backward.wait_send()


def finish(part, came, spot, dt, out, left, sem):
    rest = pltpu.make_async_copy(part.at[:, LANES:], out.at[:, LANES:], sem.at[0])
    rest.start()
    half = came.shape[0]
    width = 2 * half
    found = jnp.take_along_axis(came[...].astype(F32), jnp.broadcast_to(spot[...], (half, LANES)), axis=1)
    matched = jnp.concatenate([found, pltpu.roll(found, EDGE, 1)], axis=0)
    matched = jnp.where(iota((width, LANES), 1) < EDGE, matched, 0.0)
    rounded = matched.astype(BF16)
    copies = [rest]
    rows = width // PIECES
    for k in range(PIECES):
        at = slice(k * rows, (k + 1) * rows)
        left[at] = part[at, :LANES] + 0.5 * (matched[at] + mm(dt[at], rounded))
        here = pl.ds(k * rows, rows)
        copies.append(pltpu.make_async_copy(left.at[here], out.at[here, :LANES], sem.at[1 + k]))
        copies[-1].start()
    for copy in copies:
        copy.wait()


def solution(mesh):
    n_grp, n_peer = mesh.shape["grp"], mesh.shape["peer"]

    def per_device(state, cost, links, dyn_weight, rad_weight, cloud_weight):
        cols, width = state.shape
        half = width // 2
        held = [state.T, cost.reshape(1, cols), links, dyn_weight, rad_weight, cloud_weight]
        held = [pltpu.with_memory_space_constraint(one, pltpu.HBM) for one in held]
        parts = pl.pallas_call(
            functools.partial(kernel, n_grp, n_peer),
            out_shape=[
                jax.ShapeDtypeStruct((width, cols), F32),
                jax.ShapeDtypeStruct((half, LANES), BF16),
                jax.ShapeDtypeStruct((1, LANES), jnp.int32),
                jax.ShapeDtypeStruct((width, width), BF16),
            ],
            in_specs=[pl.BlockSpec(memory_space=pltpu.HBM)] * 6,
            out_specs=[pl.BlockSpec(memory_space=pltpu.VMEM)] * 4,
            scratch_shapes=[
                pltpu.VMEM((width, cols), F32),
                pltpu.VMEM((1, cols), jnp.int32),
                pltpu.VMEM((1, EDGE), jnp.int32),
                pltpu.VMEM((width, width), BF16),
                pltpu.VMEM((width, width), BF16),
                pltpu.VMEM((width, width), BF16),
                pltpu.VMEM((width + 16, cols), BF16),
                pltpu.VMEM((width, width), BF16),
                pltpu.VMEM((2 * width, width), BF16),
                pltpu.VMEM((SLOTS, cols), BF16),
                pltpu.VMEM((width, SLOTS), F32),
                pltpu.VMEM((width, SLOTS), F32),
                pltpu.VMEM((width, SLOTS), F32),
                pltpu.VMEM((half, LANES), BF16),
                pltpu.VMEM((half, LANES), BF16),
                pltpu.VMEM((half, LANES), BF16),
                pltpu.VMEM((half, LANES), BF16),
                pltpu.SemaphoreType.DMA((2 * PIECES,)),
                pltpu.SemaphoreType.DMA((7,)),
                pltpu.SemaphoreType.DMA((PIECES + 1,)),
                pltpu.SemaphoreType.DMA((PIECES + 1,)),
                pltpu.SemaphoreType.REGULAR,
            ],
            compiler_params=pltpu.CompilerParams(
                collective_id=0, has_side_effects=True, vmem_limit_bytes=32 * 2**20
            ),
        )(*held)
        flipped = pl.pallas_call(
            finish,
            out_shape=jax.ShapeDtypeStruct((width, cols), F32),
            in_specs=[pl.BlockSpec(memory_space=pltpu.VMEM)] * 4,
            out_specs=pl.BlockSpec(memory_space=pltpu.HBM),
            scratch_shapes=[pltpu.VMEM((width, LANES), F32), pltpu.SemaphoreType.DMA((1 + PIECES,))],
            compiler_params=pltpu.CompilerParams(vmem_limit_bytes=8 * 2**20),
        )(*[pltpu.with_memory_space_constraint(one, pltpu.VMEM) for one in parts])
        return flipped.T

    return jax.shard_map(
        per_device,
        mesh=mesh,
        in_specs=(
            P(("grp", "peer"), None),
            P(("grp", "peer")),
            P(("grp", "peer"), None),
            P(),
            P(),
            P(),
        ),
        out_specs=P(("grp", "peer"), None),
        check_vma=False,
    )
```

```python
import functools

import jax
import jax.numpy as jnp
from jax import lax
from jax.experimental import pallas as pl
from jax.experimental.pallas import tpu as pltpu
from jax.sharding import PartitionSpec as P

LEV = 48
SLOTS = 256
EDGE = 64
MICRO = 24
LANES = 128
WIDE = 256
PIECES = 2
PIECE = 48
MESH = pl.DeviceIdType.MESH
F32 = jnp.float32
BF16 = jnp.bfloat16


def mm(a, b):
    return lax.dot_general(a, b, (((1,), (0,)), ((), ())), preferred_element_type=F32)


def mm_nt(a, b):
    return lax.dot_general(a, b, (((1,), (1,)), ((), ())), preferred_element_type=F32)


def one_hot(condition):
    return jnp.where(condition, 1.0, 0.0).astype(BF16)


def iota(shape, dim):
    return lax.broadcasted_iota(jnp.int32, shape, dim)


def kernel(
    n_grp, n_peer,
    x_hbm, cost_hbm, links_hbm, wd_hbm, wr_hbm, wc_hbm,
    out, came, came_plain, spot, dt,
    x, cost, links, wd, wr, wc,
    xb, wct, wdr, pt, first, now, mask, rim_out, rim_in, plain_in, edge_out, edge_in,
    rim_sem, load_sem, send_sem, recv_sem, ready_sem,
):
    width, cols = x.shape
    first_peer = lax.axis_index("peer") == 0
    tiles = cols // LANES
    half = width // 2
    flat = lax.axis_index("grp") * n_peer + lax.axis_index("peer")
    count = n_grp * n_peer
    right = lax.rem(flat + 1, count)
    left = lax.rem(flat + count - 1, count)
    right_id = (lax.div(right, n_peer), lax.rem(right, n_peer))
    left_id = (lax.div(left, n_peer), lax.rem(left, n_peer))

    def lane_tile(t):
        return pl.ds(t * LANES, LANES)

    last = lane_tile(tiles - 1)
    packed = PIECES * PIECE
    plain = width - 2 * packed
    rim_loads = []
    for k in range(PIECES):
        for side in range(2):
            rows = pl.ds(plain + side * packed + k * PIECE, PIECE)
            rim_loads.append(pltpu.make_async_copy(x_hbm.at[rows, last], x.at[rows, last], rim_sem.at[2 * k + side]))
            rim_loads[-1].start()

    barrier = pltpu.get_barrier_semaphore()
    pl.semaphore_signal(barrier, inc=1, device_id=left_id, device_id_type=MESH)

    pl.semaphore_wait(barrier, 1)
    pl.semaphore_signal(ready_sem, inc=1, device_id=right_id, device_id_type=MESH)

    forward = [pltpu.make_async_remote_copy(
        src_ref=x_hbm.at[pl.ds(0, plain), last], dst_ref=plain_in,
        send_sem=send_sem.at[PIECES + 1], recv_sem=recv_sem.at[PIECES + 1],
        device_id=right_id, device_id_type=MESH,
    )]
    forward[0].start()

    loads = {}
    for k, (name, src, dst) in enumerate((
        ("links", links_hbm, links),
        (0, x_hbm.at[:, lane_tile(0)], x.at[:, lane_tile(0)]),
        ("cost", cost_hbm, cost),
        (1, x_hbm.at[:, pl.ds(LANES, cols - 2 * LANES)], x.at[:, pl.ds(LANES, cols - 2 * LANES)]),
        (2, x_hbm.at[pl.ds(0, plain), last], x.at[pl.ds(0, plain), last]),
        ("wc", wc_hbm, wc),
        ("wd", wd_hbm, wd),
        ("wr", wr_hbm, wr),
    )):
        loads[name] = pltpu.make_async_copy(src, dst, load_sem.at[k])
        loads[name].start()

    for k in range(PIECES):
        rim_loads[2 * k].wait()
        rim_loads[2 * k + 1].wait()
        here = pl.ds(k * PIECE, PIECE)
        upper = pltpu.roll(x[pl.ds(plain + k * PIECE, PIECE), last], EDGE, 1)
        lower = x[pl.ds(plain + packed + k * PIECE, PIECE), last]
        rim_out[here] = jnp.where(iota((PIECE, LANES), 1) < EDGE, upper, lower).astype(BF16)
        forward.append(pltpu.make_async_remote_copy(
            src_ref=rim_out.at[here], dst_ref=rim_in.at[here],
            send_sem=send_sem.at[k], recv_sem=recv_sem.at[k],
            device_id=right_id, device_id_type=MESH,
        ))
        forward[-1].start()
    backward = pltpu.make_async_remote_copy(
        src_ref=edge_out, dst_ref=edge_in, send_sem=send_sem.at[PIECES], recv_sem=recv_sem.at[PIECES],
        device_id=left_id, device_id_type=MESH,
    )

    loads["links"].wait()
    link_row = jnp.concatenate([links[...], jnp.full((1, LANES - EDGE), -LANES, jnp.int32)], axis=1)
    rows_at = iota((LANES, LANES), 0)
    match_top = one_hot(rows_at == link_row)
    match_bottom = one_hot(rows_at - EDGE == link_row)
    nowhere = jnp.zeros((1, LANES - EDGE), jnp.int32)
    spot[:1] = jnp.concatenate([links[...], nowhere], axis=1)
    spot[1:] = jnp.concatenate([links[...] + EDGE, nowhere], axis=1)

    loads[0].wait()
    xb[:width, :LANES] = x[:, :LANES].astype(BF16)
    edge_out[...] = (
        mm_nt(xb[:half, :LANES], match_top) + mm_nt(xb[half:width, :LANES], match_bottom)
    ).astype(BF16)
    loads[1].wait()
    loads[2].wait()
    for t in range(1, tiles):
        xb[:width, lane_tile(t)] = x[:, lane_tile(t)].astype(BF16)

    loads["cost"].wait()
    depth_row = cost[...]
    xb[width:, :] = jnp.broadcast_to(depth_row.astype(F32), (xb.shape[0] - width, cols)).astype(BF16)
    cloudy = jnp.where(depth_row > 0, 1.0, 0.0)
    cloudy_rows = jnp.broadcast_to(cloudy, (16, cols)).astype(BF16)
    ahead = one_hot(iota((LANES, LANES), 0) < iota((LANES, LANES), 1))
    before = jnp.zeros((1, 1), F32)
    for t in range(tiles):
        here = cloudy[:, t * LANES:(t + 1) * LANES]
        rank = mm(cloudy_rows[:, t * LANES:(t + 1) * LANES], ahead)[:1] + before
        before = before + jnp.sum(here, axis=1, keepdims=True)
        place = jnp.where(here > 0, rank.astype(jnp.int32), -1)
        pt[:, lane_tile(t)] = one_hot(iota((SLOTS, LANES), 0) == place)

    eye = one_hot(iota((width, width), 0) == iota((width, width), 1))
    loads["wc"].wait()
    wct[...] = mm_nt(eye, wc[...]).astype(BF16)

    gathered = mm_nt(xb[...], pt[...])
    first[...] = gathered[:width]
    now[...] = gathered[:width]
    slot_depth = gathered[width:width + 1].astype(jnp.int32)
    level = lax.rem(iota((width, SLOTS), 0), LEV)
    mask[...] = jnp.where(level >= LEV - slot_depth, 0.1, 0.0)

    def micro_turn(i, carry):
        forcing = mm(wct[...], now[...].astype(BF16))
        now[...] = now[...] + mask[...] * jnp.tanh(forcing)
        return carry

    lax.fori_loop(0, MICRO, micro_turn, 0)
    change = (now[...] - first[...]).astype(BF16)

    @pl.when(jnp.logical_not(first_peer))
    def _():
        pl.semaphore_wait(ready_sem, 1)
        backward.start()

    loads["wd"].wait()
    loads["wr"].wait()
    wdr[:width] = mm_nt(eye, wd[...]).astype(BF16)
    wdr[width:] = mm_nt(eye, wr[...]).astype(BF16)
    wdt = wdr[:width]
    two = mm(wdt, wdt)
    three = mm(wdt, two.astype(BF16))
    dt[...] = (0.6 * wdt.astype(F32) + 0.12 * two + 0.008 * three).astype(BF16)

    for t in range(cols // WIDE):
        at = pl.ds(t * WIDE, WIDE)
        both = mm(wdr[...], xb[:width, at])
        turned = x[:, at] + 0.2 * both[:width]
        rest = 0.25 * both[width:] + mm(change, pt[:, at])
        for _ in range(2):
            turned = turned + 0.2 * mm(wdr[:width], turned.astype(BF16))
        column = iota((width, WIDE), 1) + t * WIDE
        turned = jnp.where((column < EDGE) | (column >= cols - EDGE), 0.5 * turned, turned)
        out[:, at] = turned + rest

    backward.wait_recv()
    above, across = iota((LANES, LANES), 0), iota((LANES, LANES), 1)
    into_top = one_hot(above + EDGE == across)
    into_bottom = one_hot((above == across) & (above >= EDGE))
    matched = jnp.concatenate([mm(edge_in[...], into_top), mm(edge_in[...], into_bottom)], axis=0)
    out[:, last] = out[:, last] + 0.5 * (matched + mm(dt[...], matched.astype(BF16)))

    @pl.when(first_peer)
    def _():
        pl.semaphore_wait(ready_sem, 1)
        backward.start()

    for copy in forward:
        copy.wait_send()
    backward.wait_send()

    for copy in forward:
        copy.wait_recv()
    came[...] = rim_in[...]
    came_plain[...] = plain_in[...]


def finish(part, came, came_plain, spot, dt, out, left, sem):
    rest = pltpu.make_async_copy(part.at[:, LANES:], out.at[:, LANES:], sem.at[0])
    rest.start()
    copies = [rest]
    packed = came.shape[0]
    plain = came_plain.shape[0]

    def pick(rows, k):
        lanes = jnp.broadcast_to(spot[k:k + 1], rows.shape)
        return jnp.where(iota(rows.shape, 1) < EDGE, jnp.take_along_axis(rows, lanes, axis=1), 0.0)

    both = came[...].astype(F32)
    matched = [pick(came_plain[...], 1), pick(both, 0), pick(both, 1)]
    rounded = jnp.concatenate(matched, axis=0).astype(BF16)
    for k, (start, rows) in enumerate(((0, plain), (plain, packed), (plain + packed, packed))):
        at = pl.ds(start, rows)
        left[at] = part[at, :LANES] + 0.5 * (matched[k] + mm(dt[at], rounded))
        copies.append(pltpu.make_async_copy(left.at[at], out.at[at, :LANES], sem.at[1 + k]))
        copies[-1].start()
    for copy in copies:
        copy.wait()


def solution(mesh):
    n_grp, n_peer = mesh.shape["grp"], mesh.shape["peer"]

    def per_device(state, cost, links, dyn_weight, rad_weight, cloud_weight):
        cols, width = state.shape
        half = width // 2
        packed = PIECES * PIECE
        held = [state.T, cost.reshape(1, cols), links, dyn_weight, rad_weight, cloud_weight]
        held = [pltpu.with_memory_space_constraint(one, pltpu.HBM) for one in held]
        parts = pl.pallas_call(
            functools.partial(kernel, n_grp, n_peer),
            out_shape=[
                jax.ShapeDtypeStruct((width, cols), F32),
                jax.ShapeDtypeStruct((packed, LANES), BF16),
                jax.ShapeDtypeStruct((width - 2 * packed, LANES), F32),
                jax.ShapeDtypeStruct((2, LANES), jnp.int32),
                jax.ShapeDtypeStruct((width, width), BF16),
            ],
            in_specs=[pl.BlockSpec(memory_space=pltpu.HBM)] * 6,
            out_specs=[pl.BlockSpec(memory_space=pltpu.VMEM)] * 5,
            scratch_shapes=[
                pltpu.VMEM((width, cols), F32),
                pltpu.VMEM((1, cols), jnp.int32),
                pltpu.VMEM((1, EDGE), jnp.int32),
                pltpu.VMEM((width, width), BF16),
                pltpu.VMEM((width, width), BF16),
                pltpu.VMEM((width, width), BF16),
                pltpu.VMEM((width + 16, cols), BF16),
                pltpu.VMEM((width, width), BF16),
                pltpu.VMEM((2 * width, width), BF16),
                pltpu.VMEM((SLOTS, cols), BF16),
                pltpu.VMEM((width, SLOTS), F32),
                pltpu.VMEM((width, SLOTS), F32),
                pltpu.VMEM((width, SLOTS), F32),
                pltpu.VMEM((packed, LANES), BF16),
                pltpu.VMEM((packed, LANES), BF16),
                pltpu.VMEM((width - 2 * packed, LANES), F32),
                pltpu.VMEM((half, LANES), BF16),
                pltpu.VMEM((half, LANES), BF16),
                pltpu.SemaphoreType.DMA((2 * PIECES,)),
                pltpu.SemaphoreType.DMA((8,)),
                pltpu.SemaphoreType.DMA((PIECES + 2,)),
                pltpu.SemaphoreType.DMA((PIECES + 2,)),
                pltpu.SemaphoreType.REGULAR,
            ],
            compiler_params=pltpu.CompilerParams(
                collective_id=0, has_side_effects=True, vmem_limit_bytes=32 * 2**20
            ),
        )(*held)
        flipped = pl.pallas_call(
            finish,
            out_shape=jax.ShapeDtypeStruct((width, cols), F32),
            in_specs=[pl.BlockSpec(memory_space=pltpu.VMEM)] * 5,
            out_specs=pl.BlockSpec(memory_space=pltpu.HBM),
            scratch_shapes=[pltpu.VMEM((width, LANES), F32), pltpu.SemaphoreType.DMA((4,))],
            compiler_params=pltpu.CompilerParams(vmem_limit_bytes=8 * 2**20),
        )(*[pltpu.with_memory_space_constraint(one, pltpu.VMEM) for one in parts])
        return flipped.T

    return jax.shard_map(
        per_device,
        mesh=mesh,
        in_specs=(
            P(("grp", "peer"), None),
            P(("grp", "peer")),
            P(("grp", "peer"), None),
            P(),
            P(),
            P(),
        ),
        out_specs=P(("grp", "peer"), None),
        check_vma=False,
    )
```

```python
import functools

import jax
import jax.numpy as jnp
from jax import lax
from jax.experimental import pallas as pl
from jax.experimental.pallas import tpu as pltpu
from jax.sharding import PartitionSpec as P

LEV = 48
SLOTS = 256
EDGE = 64
MICRO = 24
LANES = 128
WIDE = 256
PIECES = 2
PIECE = 48
MESH = pl.DeviceIdType.MESH
F32 = jnp.float32
BF16 = jnp.bfloat16


def mm(a, b):
    return lax.dot_general(a, b, (((1,), (0,)), ((), ())), preferred_element_type=F32)


def mm_nt(a, b):
    return lax.dot_general(a, b, (((1,), (1,)), ((), ())), preferred_element_type=F32)


def one_hot(condition):
    return jnp.where(condition, 1.0, 0.0).astype(BF16)


def iota(shape, dim):
    return lax.broadcasted_iota(jnp.int32, shape, dim)


def kernel(
    n_grp, n_peer,
    x_hbm, cost_hbm, links_hbm, wd_hbm, wr_hbm, wc_hbm,
    out, came, spot, dt_rest,
    x, cost, links, wd, wr, wc,
    xb, wct, wdr, dt, pt, first, now, mask, rim_out, rim_in, plain_in, edge_out, edge_in,
    rim_sem, load_sem, send_sem, recv_sem, ready_sem,
):
    width, cols = x.shape
    first_peer = lax.axis_index("peer") == 0
    tiles = cols // LANES
    half = width // 2
    flat = lax.axis_index("grp") * n_peer + lax.axis_index("peer")
    count = n_grp * n_peer
    right = lax.rem(flat + 1, count)
    left = lax.rem(flat + count - 1, count)
    right_id = (lax.div(right, n_peer), lax.rem(right, n_peer))
    left_id = (lax.div(left, n_peer), lax.rem(left, n_peer))

    def lane_tile(t):
        return pl.ds(t * LANES, LANES)

    last = lane_tile(tiles - 1)
    packed = PIECES * PIECE
    plain = width - 2 * packed
    rim_loads = []
    for k in range(PIECES):
        for side in range(2):
            rows = pl.ds(plain + side * packed + k * PIECE, PIECE)
            rim_loads.append(pltpu.make_async_copy(x_hbm.at[rows, last], x.at[rows, last], rim_sem.at[2 * k + side]))
            rim_loads[-1].start()

    barrier = pltpu.get_barrier_semaphore()
    pl.semaphore_signal(barrier, inc=1, device_id=left_id, device_id_type=MESH)

    pl.semaphore_wait(barrier, 1)
    pl.semaphore_signal(ready_sem, inc=1, device_id=right_id, device_id_type=MESH)

    forward = [pltpu.make_async_remote_copy(
        src_ref=x_hbm.at[pl.ds(0, plain), last], dst_ref=plain_in,
        send_sem=send_sem.at[PIECES + 1], recv_sem=recv_sem.at[PIECES + 1],
        device_id=right_id, device_id_type=MESH,
    )]
    forward[0].start()

    loads = {}
    for k, (name, src, dst) in enumerate((
        ("links", links_hbm, links),
        (0, x_hbm.at[:, lane_tile(0)], x.at[:, lane_tile(0)]),
        ("cost", cost_hbm, cost),
        (1, x_hbm.at[:, pl.ds(LANES, cols - 2 * LANES)], x.at[:, pl.ds(LANES, cols - 2 * LANES)]),
        (2, x_hbm.at[pl.ds(0, plain), last], x.at[pl.ds(0, plain), last]),
        ("wc", wc_hbm, wc),
        ("wd", wd_hbm, wd),
        ("wr", wr_hbm, wr),
    )):
        loads[name] = pltpu.make_async_copy(src, dst, load_sem.at[k])
        loads[name].start()

    for k in range(PIECES):
        rim_loads[2 * k].wait()
        rim_loads[2 * k + 1].wait()
        here = pl.ds(k * PIECE, PIECE)
        upper = pltpu.roll(x[pl.ds(plain + k * PIECE, PIECE), last], EDGE, 1)
        lower = x[pl.ds(plain + packed + k * PIECE, PIECE), last]
        rim_out[here] = jnp.where(iota((PIECE, LANES), 1) < EDGE, upper, lower).astype(BF16)
        forward.append(pltpu.make_async_remote_copy(
            src_ref=rim_out.at[here], dst_ref=rim_in.at[here],
            send_sem=send_sem.at[k], recv_sem=recv_sem.at[k],
            device_id=right_id, device_id_type=MESH,
        ))
        forward[-1].start()
    backward = pltpu.make_async_remote_copy(
        src_ref=edge_out, dst_ref=edge_in, send_sem=send_sem.at[PIECES], recv_sem=recv_sem.at[PIECES],
        device_id=left_id, device_id_type=MESH,
    )

    loads["links"].wait()
    link_row = jnp.concatenate([links[...], jnp.full((1, LANES - EDGE), -LANES, jnp.int32)], axis=1)
    rows_at = iota((LANES, LANES), 0)
    match_top = one_hot(rows_at == link_row)
    match_bottom = one_hot(rows_at - EDGE == link_row)
    nowhere = jnp.zeros((1, LANES - EDGE), jnp.int32)
    spot[:1] = jnp.concatenate([links[...], nowhere], axis=1)
    spot[1:] = jnp.concatenate([links[...] + EDGE, nowhere], axis=1)

    loads[0].wait()
    xb[:width, :LANES] = x[:, :LANES].astype(BF16)
    edge_out[...] = (
        mm_nt(xb[:half, :LANES], match_top) + mm_nt(xb[half:width, :LANES], match_bottom)
    ).astype(BF16)
    loads[1].wait()
    loads[2].wait()
    for t in range(1, tiles):
        xb[:width, lane_tile(t)] = x[:, lane_tile(t)].astype(BF16)

    loads["cost"].wait()
    depth_row = cost[...]
    xb[width:, :] = jnp.broadcast_to(depth_row.astype(F32), (xb.shape[0] - width, cols)).astype(BF16)
    cloudy = jnp.where(depth_row > 0, 1.0, 0.0)
    cloudy_rows = jnp.broadcast_to(cloudy, (16, cols)).astype(BF16)
    ahead = one_hot(iota((LANES, LANES), 0) < iota((LANES, LANES), 1))
    before = jnp.zeros((1, 1), F32)
    for t in range(tiles):
        here = cloudy[:, t * LANES:(t + 1) * LANES]
        rank = mm(cloudy_rows[:, t * LANES:(t + 1) * LANES], ahead)[:1] + before
        before = before + jnp.sum(here, axis=1, keepdims=True)
        place = jnp.where(here > 0, rank.astype(jnp.int32), -1)
        pt[:, lane_tile(t)] = one_hot(iota((SLOTS, LANES), 0) == place)

    eye = one_hot(iota((width, width), 0) == iota((width, width), 1))
    loads["wc"].wait()
    wct[...] = mm_nt(eye, wc[...]).astype(BF16)

    gathered = mm_nt(xb[...], pt[...])
    first[...] = gathered[:width]
    now[...] = gathered[:width]
    slot_depth = gathered[width:width + 1].astype(jnp.int32)
    level = lax.rem(iota((width, SLOTS), 0), LEV)
    mask[...] = jnp.where(level >= LEV - slot_depth, 0.1, 0.0)

    def micro_turn(i, carry):
        forcing = mm(wct[...], now[...].astype(BF16))
        now[...] = now[...] + mask[...] * jnp.tanh(forcing)
        return carry

    lax.fori_loop(0, MICRO, micro_turn, 0)
    change = (now[...] - first[...]).astype(BF16)

    @pl.when(jnp.logical_not(first_peer))
    def _():
        pl.semaphore_wait(ready_sem, 1)
        backward.start()

    loads["wd"].wait()
    loads["wr"].wait()
    wdr[:width] = mm_nt(eye, wd[...]).astype(BF16)
    wdr[width:] = mm_nt(eye, wr[...]).astype(BF16)
    wdt = wdr[:width]
    two = mm(wdt, wdt)
    three = mm(wdt, two.astype(BF16))
    dt[...] = (0.6 * wdt.astype(F32) + 0.12 * two + 0.008 * three).astype(BF16)
    tail = (width, width - plain)
    dt_rest[...] = mm(dt[...], one_hot(iota(tail, 0) - plain == iota(tail, 1))).astype(BF16)

    for t in range(cols // WIDE):
        at = pl.ds(t * WIDE, WIDE)
        both = mm(wdr[...], xb[:width, at])
        turned = x[:, at] + 0.2 * both[:width]
        rest = 0.25 * both[width:] + mm(change, pt[:, at])
        for _ in range(2):
            turned = turned + 0.2 * mm(wdr[:width], turned.astype(BF16))
        column = iota((width, WIDE), 1) + t * WIDE
        turned = jnp.where((column < EDGE) | (column >= cols - EDGE), 0.5 * turned, turned)
        out[:, at] = turned + rest

    backward.wait_recv()
    above, across = iota((LANES, LANES), 0), iota((LANES, LANES), 1)
    into_top = one_hot(above + EDGE == across)
    into_bottom = one_hot((above == across) & (above >= EDGE))
    matched = jnp.concatenate([mm(edge_in[...], into_top), mm(edge_in[...], into_bottom)], axis=0)
    out[:, last] = out[:, last] + 0.5 * (matched + mm(dt[...], matched.astype(BF16)))

    @pl.when(first_peer)
    def _():
        pl.semaphore_wait(ready_sem, 1)
        backward.start()

    for copy in forward:
        copy.wait_send()
    backward.wait_send()

    forward[0].wait_recv()
    head = mm(plain_in[...].astype(BF16), match_bottom)
    out[:plain, :LANES] = out[:plain, :LANES] + 0.5 * head
    out[:, :LANES] = out[:, :LANES] + 0.5 * mm(dt[:, :plain], head.astype(BF16))
    for copy in forward[1:]:
        copy.wait_recv()
    came[...] = rim_in[...]


def finish(part, came, spot, dt_rest, out, left, sem):
    rest = pltpu.make_async_copy(part.at[:, LANES:], out.at[:, LANES:], sem.at[0])
    rest.start()
    copies = [rest]
    packed = came.shape[0]
    plain = part.shape[0] - 2 * packed
    both = came[...].astype(F32)

    def pick(k):
        lanes = jnp.broadcast_to(spot[k:k + 1], both.shape)
        return jnp.where(iota(both.shape, 1) < EDGE, jnp.take_along_axis(both, lanes, axis=1), 0.0)

    matched = [pick(0), pick(1)]
    rounded = jnp.concatenate(matched, axis=0).astype(BF16)
    for k, (start, rows) in enumerate(((0, plain), (plain, packed), (plain + packed, packed))):
        at = pl.ds(start, rows)
        turned = mm(dt_rest[at], rounded)
        if k > 0:
            turned = turned + matched[k - 1]
        left[at] = part[at, :LANES] + 0.5 * turned
        copies.append(pltpu.make_async_copy(left.at[at], out.at[at, :LANES], sem.at[1 + k]))
        copies[-1].start()
    for copy in copies:
        copy.wait()


def solution(mesh):
    n_grp, n_peer = mesh.shape["grp"], mesh.shape["peer"]

    def per_device(state, cost, links, dyn_weight, rad_weight, cloud_weight):
        cols, width = state.shape
        half = width // 2
        packed = PIECES * PIECE
        held = [state.T, cost.reshape(1, cols), links, dyn_weight, rad_weight, cloud_weight]
        held = [pltpu.with_memory_space_constraint(one, pltpu.HBM) for one in held]
        parts = pl.pallas_call(
            functools.partial(kernel, n_grp, n_peer),
            out_shape=[
                jax.ShapeDtypeStruct((width, cols), F32),
                jax.ShapeDtypeStruct((packed, LANES), BF16),
                jax.ShapeDtypeStruct((2, LANES), jnp.int32),
                jax.ShapeDtypeStruct((width, 2 * packed), BF16),
            ],
            in_specs=[pl.BlockSpec(memory_space=pltpu.HBM)] * 6,
            out_specs=[pl.BlockSpec(memory_space=pltpu.VMEM)] * 4,
            scratch_shapes=[
                pltpu.VMEM((width, cols), F32),
                pltpu.VMEM((1, cols), jnp.int32),
                pltpu.VMEM((1, EDGE), jnp.int32),
                pltpu.VMEM((width, width), BF16),
                pltpu.VMEM((width, width), BF16),
                pltpu.VMEM((width, width), BF16),
                pltpu.VMEM((width + 16, cols), BF16),
                pltpu.VMEM((width, width), BF16),
                pltpu.VMEM((2 * width, width), BF16),
                pltpu.VMEM((width, width), BF16),
                pltpu.VMEM((SLOTS, cols), BF16),
                pltpu.VMEM((width, SLOTS), F32),
                pltpu.VMEM((width, SLOTS), F32),
                pltpu.VMEM((width, SLOTS), F32),
                pltpu.VMEM((packed, LANES), BF16),
                pltpu.VMEM((packed, LANES), BF16),
                pltpu.VMEM((width - 2 * packed, LANES), F32),
                pltpu.VMEM((half, LANES), BF16),
                pltpu.VMEM((half, LANES), BF16),
                pltpu.SemaphoreType.DMA((2 * PIECES,)),
                pltpu.SemaphoreType.DMA((8,)),
                pltpu.SemaphoreType.DMA((PIECES + 2,)),
                pltpu.SemaphoreType.DMA((PIECES + 2,)),
                pltpu.SemaphoreType.REGULAR,
            ],
            compiler_params=pltpu.CompilerParams(
                collective_id=0, has_side_effects=True, vmem_limit_bytes=32 * 2**20
            ),
        )(*held)
        flipped = pl.pallas_call(
            finish,
            out_shape=jax.ShapeDtypeStruct((width, cols), F32),
            in_specs=[pl.BlockSpec(memory_space=pltpu.VMEM)] * 4,
            out_specs=pl.BlockSpec(memory_space=pltpu.HBM),
            scratch_shapes=[pltpu.VMEM((width, LANES), F32), pltpu.SemaphoreType.DMA((4,))],
            compiler_params=pltpu.CompilerParams(vmem_limit_bytes=8 * 2**20),
        )(*[pltpu.with_memory_space_constraint(one, pltpu.VMEM) for one in parts])
        return flipped.T

    return jax.shard_map(
        per_device,
        mesh=mesh,
        in_specs=(
            P(("grp", "peer"), None),
            P(("grp", "peer")),
            P(("grp", "peer"), None),
            P(),
            P(),
            P(),
        ),
        out_specs=P(("grp", "peer"), None),
        check_vma=False,
    )
```
